256 devices in a mesh: pair: 32 (over y_lo, z, core), freq: 8 (over x, y_hi).
Axes of the slice: x: 4, y: 4 (y_hi: 2, y_lo: 2; y = y_hi * 2 + y_lo), z: 8, core: 2. Of those that a mesh axis runs over, the one named last changes fastest.
Arguments:
- home_spectra: bfloat16 [8192, 2, 8, 512], P(('pair', 'freq')), may hold values from -6 to 6
- travel_spectra: bfloat16 [8192, 2, 8, 512], P(('pair', 'freq')), may hold values from -6 to 6
- rotation: int32 [1], replicated, may hold values from 0 to 31
Outputs:
- correlation: bfloat16 [1, 32, 256, 256, 128], P(None, 'pair', None, 'freq')
The draws below stay inside these ranges and needn't reach their ends.
All inputs are finite; a program needn't handle non-finite values.
Results may differ from the reference program's by a relative error of at most 0.0058.
Values may be sent and summed in bfloat16 or wider, within the bound.
No kernel may reach another device: no remote copies, remote signals or barrier semaphores. Data moves between devices by JAX's collectives and lax.ppermute only.
A program may use at most 128 MiB of HBM per device.

```python
import math
import jax
import jax.numpy as jnp
from jax import lax

BLOCK = 256
FREQS = 512
LAGS = 128
WINDOWS = 8
ROUNDS = 1
HALF_CH = 8192
N_PAIR = 32


def block_levels(key, extent, pieces, smallest, largest):
    def one(dim, parts):
        steps = jax.random.uniform(jax.random.fold_in(jax.random.fold_in(key, 6), dim), (parts,), jnp.float32, smallest / len(pieces), largest / len(pieces))
        return jnp.repeat(jnp.exp(steps), extent[dim] // parts).reshape((-1,) + (1,) * (len(extent) - dim - 1))

    level = one(*pieces[0])
    for cut in pieces[1:]:
        level = level * one(*cut)
    return level


def noise(rng, extent, spread, bound, pieces=(), held_as=jnp.bfloat16):
    array = jax.random.normal(rng, extent, jnp.float32) * spread
    if len(pieces) > 0:
        array = block_levels(rng, extent, pieces, -0.22, 0.18) * array
    return jnp.clip(array, min=-bound, max=bound).astype(held_as)


def setup_inputs(seed: int = 0) -> dict:
    keys = jax.random.split(jax.random.key(seed), 4)
    return {
        "home_spectra": noise(keys[0], (HALF_CH, 2, WINDOWS, FREQS), 1.0, 6.0, ((0, 256),)),
        "travel_spectra": noise(keys[1], (HALF_CH, 2, WINDOWS, FREQS), 1.0, 6.0, ((0, 256),)),
        "rotation": jax.random.randint(keys[2], (1,), 0, N_PAIR).astype(jnp.int32),
    }


def make_table(freq_count, lag_count, window_count):
    freq_index = jnp.arange(freq_count, dtype=jnp.int32)[:, None]
    lag_index = jnp.arange(lag_count, dtype=jnp.int32)[None, :] - lag_count // 2
    phase_step = freq_index * lag_index % (2 * freq_count)
    angles = phase_step.astype(jnp.float32) * (math.pi / freq_count)
    norm_scale = 1.0 / math.sqrt(2.0 * window_count * freq_count)
    return jnp.stack([jnp.cos(angles) * norm_scale, -jnp.sin(angles) * norm_scale], axis=0).astype(jnp.bfloat16)

def correlate(home_block, travel_block, lag_table):
    freq_count = home_block.shape[3]
    band_width = min(128, freq_count)
    turned = jnp.stack([-travel_block[:, 1], travel_block[:, 0]], axis=1)
    partner_terms = jnp.stack([travel_block, turned], axis=0)
    summed = jnp.zeros((home_block.shape[0], travel_block.shape[0], lag_table.shape[2]), jnp.float32)
    for begin in range(0, freq_count, band_width):
        home_band = home_block[..., begin:begin + band_width].astype(jnp.float32)
        partner_band = partner_terms[..., begin:begin + band_width].astype(jnp.float32)
        cross = jnp.einsum('hcwf,ptcwf->hptf', home_band, partner_band).astype(jnp.bfloat16)
        table_band = lag_table[:, begin:begin + band_width].astype(jnp.float32)
        summed = summed + jnp.einsum('hptf,pfl->htl', cross.astype(jnp.float32), table_band)
    return summed

def reference(home_spectra, travel_spectra, rotation):
    lag_table = make_table(FREQS, LAGS, WINDOWS)
    offset = rotation[0].astype(jnp.int32)
    rounds_out = []
    for round_index in range(ROUNDS):

        def per_block(block_index):
            home_block = lax.dynamic_slice_in_dim(home_spectra, (block_index * BLOCK).astype(jnp.int32), BLOCK, 0)
            partner = ((block_index - offset - round_index) % N_PAIR).astype(jnp.int32)
            travel_block = lax.dynamic_slice_in_dim(travel_spectra, (partner * BLOCK).astype(jnp.int32), BLOCK, 0)
            return correlate(home_block, travel_block, lag_table).astype(jnp.bfloat16)
        rounds_out.append(lax.map(per_block, jnp.arange(N_PAIR, dtype=jnp.int32)))
    return jnp.stack(rounds_out, axis=0)
```

```python
import functools
import math

import jax
import jax.numpy as jnp
from jax import lax
from jax.experimental import pallas as pl
from jax.experimental.pallas import tpu as pltpu
from jax.sharding import PartitionSpec as P

LAGS = 128
BAND = 128
RUN = 16


def make_table(freq_count, lag_count, window_count):
    freq_index = jnp.arange(freq_count, dtype=jnp.int32)[None, :]
    lag_index = jnp.arange(lag_count, dtype=jnp.int32)[:, None] - lag_count // 2
    phase_step = freq_index * lag_index % (2 * freq_count)
    angles = phase_step.astype(jnp.float32) * (math.pi / freq_count)
    norm_scale = 1.0 / math.sqrt(2.0 * window_count * freq_count)
    table = jnp.stack([jnp.cos(angles) * norm_scale, -jnp.sin(angles) * norm_scale], axis=0)
    bands = freq_count // BAND
    table = table.astype(jnp.bfloat16).reshape(2, lag_count, bands, BAND)
    return table.transpose(2, 1, 0, 3).reshape(bands, lag_count, 2 * BAND)


def along(value, axis, by):
    count = lax.axis_size(axis)
    return lax.ppermute(value, axis, [(i, (i + by) % count) for i in range(count)])


def ring(value, step):
    return along(value, "freq", 2 * step)


def across(value):
    return lax.ppermute(value, "freq", [(i, i ^ 1) for i in range(lax.axis_size("freq"))])


def gather_home(own):
    half = own.shape[0] // 2
    other = across(own)
    left = ring(own, 1)
    right = ring(own, -1)
    far_low = ring(left[:half], 1)
    far_high = ring(right[half:], -1)
    other_left_low = ring(other[:half], 1)
    other_right_high = ring(other[half:], -1)
    other_left_high = across(left[half:])
    other_right_low = across(right[:half])
    other_far_low = ring(other_left_low, 1)
    other_far_high = ring(other_right_high, -1)
    return [
        own,
        left,
        right,
        far_low,
        far_high,
        other,
        other_left_low,
        other_left_high,
        other_right_low,
        other_right_high,
        other_far_low,
        other_far_high,
    ]


def home_places():
    me = lax.axis_index("freq")
    place, row = me // 2, me % 2
    found = []
    for side in (0, 1):
        for step in (0, -1, 1, 2):
            found.append(((place + step) % 4) * 2 + (row ^ side))
    return jnp.stack(found).astype(jnp.int32)


def kernel(places, *refs, piece_count):
    pieces, travel, table = refs[:piece_count], refs[piece_count], refs[piece_count + 1]
    out, wide, weights, terms, cross, total, turned = refs[piece_count + 2 :]
    channels, term_count, band = travel.shape
    home_count = weights.shape[2] // 2
    half = term_count // 2
    step = pl.program_id(0)

    begin = 0
    for piece in pieces:
        rows = piece.shape[0] * term_count
        wide[begin : begin + rows] = piece[...].astype(jnp.float32).reshape(rows, band)
        begin += rows
    for k in range(term_count):
        rows = wide[pl.ds(k, home_count, stride=term_count), :].astype(jnp.bfloat16).T
        weights[k, :, :home_count] = rows
        if k < half:
            weights[half + k, :, home_count:] = -rows
        else:
            weights[k - half, :, home_count:] = rows

    wide_terms = term_count * RUN
    spread_row = lax.broadcasted_iota(jnp.int32, (term_count, wide_terms), 0)
    spread_lane = lax.broadcasted_iota(jnp.int32, (term_count, wide_terms), 1)
    spread = jnp.where(spread_lane // RUN == spread_row, 1.0, 0.0).astype(jnp.bfloat16)
    row = lax.broadcasted_iota(jnp.int32, (band, wide_terms), 0)
    lane = lax.broadcasted_iota(jnp.int32, (band, wide_terms), 1)
    diagonal = jnp.where(row % RUN == lane % RUN, 1.0, 0.0).astype(jnp.bfloat16)
    for t in range(channels):
        repeated = lax.dot_general(
            travel[t], spread, (((0,), (0,)), ((), ())), preferred_element_type=jnp.float32
        )
        terms[t] = repeated.astype(jnp.bfloat16) * diagonal

    for at in range(0, band, RUN):
        weight = weights[:, at : at + RUN, :].reshape(wide_terms, 2 * home_count)
        term = terms[:, at : at + RUN, :].reshape(channels * RUN, wide_terms)
        found = jnp.dot(term, weight, preferred_element_type=jnp.float32).astype(jnp.bfloat16)
        cross[:, 0, at : at + RUN, :] = found[:, :home_count].reshape(channels, RUN, home_count)
        cross[:, 1, at : at + RUN, :] = found[:, home_count:].reshape(channels, RUN, home_count)

    for t in range(channels):
        terms_of_t = cross[t].reshape(2 * band, home_count)
        product = jnp.dot(table[0], terms_of_t, preferred_element_type=jnp.float32)
        total[t] = jnp.where(step == 0, 0.0, total[t]) + product

    @pl.when(step == pl.num_programs(0) - 1)
    def _():
        for t in range(channels):
            turned[t * home_count : (t + 1) * home_count] = (
                total[t].astype(jnp.bfloat16).T.astype(jnp.float32)
            )
        block = home_count // places.shape[0]
        for place in range(places.shape[0]):
            first = places[place] * block

            def write(i, carry):
                rows = turned[pl.ds(place * block + i, channels, stride=home_count), :]
                out[first + i] = rows.astype(jnp.bfloat16)
                return carry

            lax.fori_loop(0, block, write, 0, unroll=16)


def correlate(pieces, travel, table, places):
    channels, term_count, freq_count = travel.shape
    home_count = sum(piece.shape[0] for piece in pieces)
    bands, lag_count, _ = table.shape
    spec = lambda n: pl.BlockSpec((n, term_count, BAND), lambda c: (0, 0, c))
    return pl.pallas_call(
        functools.partial(kernel, piece_count=len(pieces)),
        grid=(bands,),
        in_specs=[pl.BlockSpec(memory_space=pltpu.SMEM)]
        + [spec(piece.shape[0]) for piece in pieces]
        + [spec(channels), pl.BlockSpec((1, lag_count, 2 * BAND), lambda c: (c, 0, 0))],
        out_specs=pl.BlockSpec((home_count, channels, lag_count), lambda c: (0, 0, 0)),
        out_shape=jax.ShapeDtypeStruct((home_count, channels, lag_count), jnp.bfloat16),
        scratch_shapes=[
            pltpu.VMEM((home_count * term_count, BAND), jnp.float32),
            pltpu.VMEM((term_count, BAND, 2 * home_count), jnp.bfloat16),
            pltpu.VMEM((channels, BAND, term_count * RUN), jnp.bfloat16),
            pltpu.VMEM((channels, 2, BAND, home_count), jnp.bfloat16),
            pltpu.VMEM((channels, lag_count, home_count), jnp.float32),
            pltpu.VMEM((home_count * channels, lag_count), jnp.float32),
        ],
        compiler_params=pltpu.CompilerParams(vmem_limit_bytes=56 * 2**20),
        cost_estimate=pl.CostEstimate(
            flops=2 * channels * home_count * freq_count * (16 * term_count * 2 + 2 * lag_count),
            bytes_accessed=8 * 2**20,
            transcendentals=0,
        ),
    )(places, *pieces, travel, table)


def per_device(home_spectra, travel_spectra, rotation):
    own_count, parts, window_count, freq_count = home_spectra.shape
    pair_count = lax.axis_size("pair")
    home = home_spectra.reshape(own_count, parts * window_count, freq_count)
    travel = travel_spectra.reshape(own_count, parts * window_count, freq_count)
    table = make_table(freq_count, LAGS, window_count)

    def exchange(offset):
        def branch(home, travel):
            moved = along(travel, "pair", offset) if offset else travel
            return gather_home(home), moved

        return branch

    pieces, moved = lax.switch(
        rotation[0], [exchange(offset) for offset in range(pair_count)], home, travel
    )
    return correlate(pieces, moved, table, home_places())[None, None]


def solution(mesh):
    in_specs = (P(("pair", "freq"), None, None, None), P(("pair", "freq"), None, None, None), P())
    out_specs = P(None, "pair", None, "freq", None)
    return jax.shard_map(
        per_device, mesh=mesh, in_specs=in_specs, out_specs=out_specs, check_vma=False
    )
```

```python
import functools
import math

import jax
import jax.numpy as jnp
from jax import lax
from jax.experimental import pallas as pl
from jax.experimental.pallas import tpu as pltpu
from jax.sharding import PartitionSpec as P

LAGS = 128
BAND = 128
RUN = 8


def make_table(freq_count, lag_count, window_count):
    freq_index = jnp.arange(freq_count, dtype=jnp.int32)[None, :]
    lag_index = jnp.arange(lag_count, dtype=jnp.int32)[:, None] - lag_count // 2
    phase_step = freq_index * lag_index % (2 * freq_count)
    angles = phase_step.astype(jnp.float32) * (math.pi / freq_count)
    norm_scale = 1.0 / math.sqrt(2.0 * window_count * freq_count)
    table = [jnp.cos(angles) * norm_scale, -jnp.sin(angles) * norm_scale]
    return jnp.concatenate(table, axis=1).astype(jnp.bfloat16)


def along(value, axis, by):
    count = lax.axis_size(axis)
    return lax.ppermute(value, axis, [(i, (i + by) % count) for i in range(count)])


def ring(value, step):
    return along(value, "freq", 2 * step)


def across(value):
    return lax.ppermute(value, "freq", [(i, i ^ 1) for i in range(lax.axis_size("freq"))])


def places_of(side):
    me = lax.axis_index("freq")
    place, row = me // 2, me % 2
    found = [((place + step) % 4) * 2 + (row ^ side) for step in (0, -1, 1, 2)]
    return jnp.stack(found).astype(jnp.int32)


def moved(value, index, choices, unit):
    def branch(by):
        return lambda v: along(v, "pair", by * unit) if by else v

    return lax.switch(index, [branch(by) for by in choices], value)


def kernel(places, *refs, piece_count, first):
    pieces, travel, table = refs[:piece_count], refs[piece_count], refs[piece_count + 1]
    if first:
        out, terms, wide, weights, cross, turned, ready, sems = refs[piece_count + 2 :]
    else:
        terms = travel
        out, wide, weights, cross, turned, ready, sems = refs[piece_count + 3 :]
    _, term_count, band = pieces[0].shape
    channels, _, _, home_count = cross.shape
    half = term_count // 2
    groups = band // RUN
    lanes = term_count * RUN
    step = pl.program_id(0)

    begin = 0
    for piece in pieces:
        rows = piece.shape[0] * term_count
        wide[begin : begin + rows] = piece[...].astype(jnp.float32).reshape(rows, band)
        begin += rows

    def of_term(k):
        rows = wide[pl.ds(k, home_count, stride=term_count), :]
        return rows.astype(jnp.bfloat16).T.astype(jnp.float32).reshape(groups, RUN, home_count)

    for k in range(0, term_count, 2):
        two = jnp.concatenate([of_term(k), of_term(k + 1)], axis=1).astype(jnp.bfloat16)
        weights[:, k * RUN : (k + 2) * RUN, :home_count] = two
        if k < half:
            weights[:, (k + half) * RUN : (k + half + 2) * RUN, home_count:] = -two
        else:
            weights[:, (k - half) * RUN : (k - half + 2) * RUN, home_count:] = two

    if first:
        many = lanes // term_count
        blocks = channels // many
        sides = [travel[c : c + many].reshape(lanes, band).T for c in range(0, channels, many)]
        side = jnp.concatenate(sides, axis=0)
        spread_row = lax.broadcasted_iota(jnp.int32, (lanes, 2 * lanes), 0)
        spread_lane = lax.broadcasted_iota(jnp.int32, (lanes, 2 * lanes), 1)
        row = lax.broadcasted_iota(jnp.int32, (2 * RUN, lanes), 0)
        lane = lax.broadcasted_iota(jnp.int32, (2 * RUN, lanes), 1)
        diagonal = jnp.where(row % RUN == lane % RUN, 1.0, 0.0).astype(jnp.bfloat16)
        for j in range(many // 2):
            chosen = spread_row == 2 * j * term_count + spread_lane // RUN
            spread = jnp.where(chosen, 1.0, 0.0).astype(jnp.bfloat16)
            found = jnp.dot(side, spread, preferred_element_type=jnp.float32)
            found = found.reshape(blocks, groups, RUN, 2 * lanes)
            found = jnp.concatenate([found[..., :lanes], found[..., lanes:]], axis=2)
            found = found.astype(jnp.bfloat16) * diagonal
            for c in range(blocks):
                at = (c * many + 2 * j) * RUN
                terms[:, at : at + 2 * RUN, :] = found[c]

    for g in range(0, groups, 2):
        two = [
            jnp.dot(terms[g + i], weights[g + i], preferred_element_type=jnp.float32)
            for i in range(2)
        ]
        two = [x.reshape(channels, RUN, 2 * home_count) for x in two]
        found = jnp.concatenate(two, axis=1).astype(jnp.bfloat16)
        to = pl.ds(pl.multiple_of(step * band + g * RUN, 2 * RUN), 2 * RUN)
        cross[:, 0, to, :] = found[..., :home_count]
        cross[:, 1, to, :] = found[..., home_count:]

    @pl.when(step == pl.num_programs(0) - 1)
    def _():
        for t in range(0, channels, 2):
            two = [cross[t + i].reshape(-1, home_count) for i in range(2)]
            product = jnp.dot(
                table[...], jnp.concatenate(two, axis=1), preferred_element_type=jnp.float32
            )
            turned[t * home_count : (t + 2) * home_count] = (
                product.astype(jnp.bfloat16).T.astype(jnp.float32)
            )
        block = home_count // piece_count
        copies = []
        for b in range(piece_count):
            for i in range(b * block, (b + 1) * block):
                rows = turned[pl.ds(i, channels, stride=home_count), :]
                ready[i] = rows.astype(jnp.bfloat16)
            to = pl.ds(pl.multiple_of(places[b] * block, block), block)
            copies.append(
                pltpu.make_async_copy(ready.at[pl.ds(b * block, block)], out.at[to], sems.at[b])
            )
            copies[-1].start()
        for copy in copies:
            copy.wait()


def correlate(pieces, travel, table, places, home_total, so_far=None):
    first = so_far is None
    _, term_count, freq_count = pieces[0].shape
    home_count = sum(piece.shape[0] for piece in pieces)
    lag_count = table.shape[0]
    channels = travel.shape[0] if first else travel.shape[1] // RUN
    lanes = term_count * RUN
    spec = lambda n: pl.BlockSpec((n, term_count, BAND), lambda c: (0, 0, c))
    term_spec = pl.BlockSpec((BAND // RUN, channels * RUN, lanes), lambda c: (c, 0, 0))
    term_shape = jax.ShapeDtypeStruct((freq_count // RUN, channels * RUN, lanes), jnp.bfloat16)
    out_spec = pl.BlockSpec(memory_space=pl.ANY)
    out_shape = jax.ShapeDtypeStruct((home_total, channels, lag_count), jnp.bfloat16)
    earlier = [] if first else [so_far]
    return pl.pallas_call(
        functools.partial(kernel, piece_count=len(pieces), first=first),
        grid=(freq_count // BAND,),
        in_specs=[pl.BlockSpec(memory_space=pltpu.SMEM)]
        + [spec(piece.shape[0]) for piece in pieces]
        + [spec(channels) if first else term_spec]
        + [pl.BlockSpec((lag_count, 2 * freq_count), lambda c: (0, 0))]
        + [out_spec] * len(earlier),
        out_specs=[out_spec, term_spec] if first else out_spec,
        out_shape=[out_shape, term_shape] if first else out_shape,
        scratch_shapes=[
            pltpu.VMEM((home_count * term_count, BAND), jnp.float32),
            pltpu.VMEM((BAND // RUN, lanes, 2 * home_count), jnp.bfloat16),
            pltpu.VMEM((channels, 2, freq_count, home_count), jnp.bfloat16),
            pltpu.VMEM((home_count * channels, lag_count), jnp.float32),
            pltpu.VMEM((home_count, channels, lag_count), jnp.bfloat16),
            pltpu.SemaphoreType.DMA((len(pieces),)),
        ],
        input_output_aliases={} if first else {len(pieces) + 3: 0},
        compiler_params=pltpu.CompilerParams(vmem_limit_bytes=32 * 2**20),
        cost_estimate=pl.CostEstimate(
            flops=2 * channels * home_count * freq_count * (32 * term_count + 2 * lag_count),
            bytes_accessed=8 * 2**20,
            transcendentals=0,
        ),
    )(places, *pieces, travel, table, *earlier)


def per_device(home_spectra, travel_spectra, rotation):
    own_count, parts, window_count, freq_count = home_spectra.shape
    home_total = own_count * lax.axis_size("freq")
    own = home_spectra.reshape(own_count, parts * window_count, freq_count)
    travel = travel_spectra.reshape(own_count, parts * window_count, freq_count)
    table = make_table(freq_count, LAGS, window_count)

    far = ring(own, 2)
    left = ring(own, 1)
    right = ring(own, -1)
    other = across(own)
    fine = rotation[0] & 3
    coarse = ((rotation[0] + 1) >> 2) & 7
    travel = moved(travel, fine, (0, 1, 2, -1), 1)
    travel = moved(travel, coarse, (0, 1, 2, 3, 4, 5, 6, 7), 4)
    far, left, right, other, travel = lax.optimization_barrier((far, left, right, other, travel))

    other_left = ring(other, 1)
    other_right = ring(other, -1)
    other_far = across(far)
    row = [own, left, right, far]
    found, terms = correlate(row, travel, table, places_of(0), home_total)
    others = [other, other_left, other_right, other_far]
    found = correlate(others, terms, table, places_of(1), home_total, found)
    return found[None, None]


def solution(mesh):
    in_specs = (P(("pair", "freq"), None, None, None), P(("pair", "freq"), None, None, None), P())
    out_specs = P(None, "pair", None, "freq", None)
    return jax.shard_map(
        per_device, mesh=mesh, in_specs=in_specs, out_specs=out_specs, check_vma=False
    )
```

```python
import functools
import math

import jax
import jax.numpy as jnp
from jax import lax
from jax.experimental import pallas as pl
from jax.experimental.pallas import tpu as pltpu
from jax.sharding import PartitionSpec as P

LAGS = 128
BAND = 128
RUN = 8
PAD = 8


def make_table(freq_count, lag_count, window_count):
    freq_index = jnp.arange(freq_count, dtype=jnp.int32)[None, :]
    lag_index = jnp.arange(lag_count, dtype=jnp.int32)[:, None] - lag_count // 2
    phase_step = freq_index * lag_index % (2 * freq_count)
    angles = phase_step.astype(jnp.float32) * (math.pi / freq_count)
    norm_scale = 1.0 / math.sqrt(2.0 * window_count * freq_count)
    table = [jnp.cos(angles) * norm_scale, -jnp.sin(angles) * norm_scale]
    return jnp.concatenate(table, axis=1).astype(jnp.bfloat16)


def along(value, axis, by):
    count = lax.axis_size(axis)
    return lax.ppermute(value, axis, [(i, (i + by) % count) for i in range(count)])


def ring(value, step):
    return along(value, "freq", 2 * step)


def across(value):
    return lax.ppermute(value, "freq", [(i, i ^ 1) for i in range(lax.axis_size("freq"))])


def places_of(side):
    me = lax.axis_index("freq")
    place, row = me // 2, me % 2
    found = [((place + step) % 4) * 2 + (row ^ side) for step in (0, -1, 1, 2)]
    return jnp.stack(found).astype(jnp.int32)


def moved(value, by):
    count = lax.axis_size("pair")
    branch = lambda step: lambda v: along(v, "pair", step) if step else v
    return lax.switch(by, [branch(step) for step in range(count)], value)


def kernel(places, *refs, piece_count, first):
    pieces, travel, table = refs[:piece_count], refs[piece_count], refs[piece_count + 1]
    if first:
        out, terms, wide, weights, cross, turned, ready, sems = refs[piece_count + 2 :]
    else:
        terms = travel
        out, wide, weights, cross, turned, ready, sems = refs[piece_count + 3 :]
    _, term_count, band = pieces[0].shape
    channels, _, _, home_count = cross.shape
    half = term_count // 2
    groups = band // RUN
    lanes = term_count * RUN
    step = pl.program_id(0)

    pitch = term_count + PAD
    begin = 0
    for piece in pieces:
        for i in range(piece.shape[0]):
            wide[begin : begin + term_count] = piece[i].astype(jnp.float32)
            begin += pitch

    def of_term(k):
        rows = wide[pl.ds(k, home_count, stride=pitch), :]
        return rows.T.reshape(groups, RUN, home_count)

    for k in range(0, term_count, 2):
        two = jnp.concatenate([of_term(k), of_term(k + 1)], axis=1).astype(jnp.bfloat16)
        weights[:, k * RUN : (k + 2) * RUN, :home_count] = two
        if k < half:
            weights[:, (k + half) * RUN : (k + half + 2) * RUN, home_count:] = -two
        else:
            weights[:, (k - half) * RUN : (k - half + 2) * RUN, home_count:] = two

    if first:
        many = lanes // term_count
        blocks = channels // many
        sides = [travel[c : c + many].reshape(lanes, band).T for c in range(0, channels, many)]
        side = jnp.concatenate(sides, axis=0)
        spread_row = lax.broadcasted_iota(jnp.int32, (lanes, 2 * lanes), 0)
        spread_lane = lax.broadcasted_iota(jnp.int32, (lanes, 2 * lanes), 1)
        row = lax.broadcasted_iota(jnp.int32, (2 * RUN, lanes), 0)
        lane = lax.broadcasted_iota(jnp.int32, (2 * RUN, lanes), 1)
        diagonal = jnp.where(row % RUN == lane % RUN, 1.0, 0.0).astype(jnp.bfloat16)
        for j in range(many // 2):
            chosen = spread_row == 2 * j * term_count + spread_lane // RUN
            spread = jnp.where(chosen, 1.0, 0.0).astype(jnp.bfloat16)
            found = jnp.dot(side, spread, preferred_element_type=jnp.float32)
            found = found.reshape(blocks, groups, RUN, 2 * lanes)
            found = jnp.concatenate([found[..., :lanes], found[..., lanes:]], axis=2)
            found = found.astype(jnp.bfloat16) * diagonal
            for c in range(blocks):
                at = (c * many + 2 * j) * RUN
                terms[:, at : at + 2 * RUN, :] = found[c]

    for g in range(0, groups, 2):
        two = [
            jnp.dot(terms[g + i], weights[g + i], preferred_element_type=jnp.float32)
            for i in range(2)
        ]
        two = [x.reshape(channels, RUN, 2 * home_count) for x in two]
        found = jnp.concatenate(two, axis=1).astype(jnp.bfloat16)
        to = pl.ds(pl.multiple_of(step * band + g * RUN, 2 * RUN), 2 * RUN)
        cross[:, 0, to, :] = found[..., :home_count]
        cross[:, 1, to, :] = found[..., home_count:]

    @pl.when(step == pl.num_programs(0) - 1)
    def _():
        for t in range(0, channels, 2):
            two = [cross[t + i].reshape(-1, home_count) for i in range(2)]
            product = jnp.dot(
                table[...], jnp.concatenate(two, axis=1), preferred_element_type=jnp.float32
            )
            product = product.astype(jnp.bfloat16).T.astype(jnp.float32)
            for i in range(2):
                begin = (t + i) * (home_count + PAD)
                turned[begin : begin + home_count] = product[i * home_count : (i + 1) * home_count]
        block = home_count // piece_count
        copies = []
        for b in range(piece_count):

            def finish(i, carry):
                rows = turned[pl.ds(b * block + i, channels, stride=home_count + PAD), :]
                ready[b * block + i] = rows.astype(jnp.bfloat16)
                return carry

            lax.fori_loop(0, block, finish, 0, unroll=8)
            to = pl.ds(pl.multiple_of(places[b] * block, block), block)
            copies.append(
                pltpu.make_async_copy(ready.at[pl.ds(b * block, block)], out.at[to], sems.at[b])
            )
            copies[-1].start()
        for copy in copies:
            copy.wait()


def correlate(pieces, travel, table, places, home_total, so_far=None):
    first = so_far is None
    _, term_count, freq_count = pieces[0].shape
    home_count = sum(piece.shape[0] for piece in pieces)
    lag_count = table.shape[0]
    channels = travel.shape[0] if first else travel.shape[1] // RUN
    lanes = term_count * RUN
    spec = lambda n: pl.BlockSpec((n, term_count, BAND), lambda c: (0, 0, c))
    term_spec = pl.BlockSpec((BAND // RUN, channels * RUN, lanes), lambda c: (c, 0, 0))
    term_shape = jax.ShapeDtypeStruct((freq_count // RUN, channels * RUN, lanes), jnp.bfloat16)
    out_spec = pl.BlockSpec(memory_space=pl.ANY)
    out_shape = jax.ShapeDtypeStruct((home_total, channels, lag_count), jnp.bfloat16)
    earlier = [] if first else [so_far]
    return pl.pallas_call(
        functools.partial(kernel, piece_count=len(pieces), first=first),
        grid=(freq_count // BAND,),
        in_specs=[pl.BlockSpec(memory_space=pltpu.SMEM)]
        + [spec(piece.shape[0]) for piece in pieces]
        + [spec(channels) if first else term_spec]
        + [pl.BlockSpec((lag_count, 2 * freq_count), lambda c: (0, 0))]
        + [out_spec] * len(earlier),
        out_specs=[out_spec, term_spec] if first else out_spec,
        out_shape=[out_shape, term_shape] if first else out_shape,
        scratch_shapes=[
            pltpu.VMEM((home_count * (term_count + PAD), BAND), jnp.float32),
            pltpu.VMEM((BAND // RUN, lanes, 2 * home_count), jnp.bfloat16),
            pltpu.VMEM((channels, 2, freq_count, home_count), jnp.bfloat16),
            pltpu.VMEM(((home_count + PAD) * channels, lag_count), jnp.float32),
            pltpu.VMEM((home_count, channels, lag_count), jnp.bfloat16),
            pltpu.SemaphoreType.DMA((len(pieces),)),
        ],
        input_output_aliases={} if first else {len(pieces) + 3: 0},
        compiler_params=pltpu.CompilerParams(vmem_limit_bytes=32 * 2**20),
        cost_estimate=pl.CostEstimate(
            flops=2 * channels * home_count * freq_count * (32 * term_count + 2 * lag_count),
            bytes_accessed=8 * 2**20,
            transcendentals=0,
        ),
    )(places, *pieces, travel, table, *earlier)


def per_device(home_spectra, travel_spectra, rotation):
    own_count, parts, window_count, freq_count = home_spectra.shape
    home_total = own_count * lax.axis_size("freq")
    own = home_spectra.reshape(own_count, parts * window_count, freq_count)
    travel = travel_spectra.reshape(own_count, parts * window_count, freq_count)
    table = make_table(freq_count, LAGS, window_count)

    far = ring(own, 2)
    left = ring(own, 1)
    right = ring(own, -1)
    other = across(own)
    travel = moved(travel, rotation[0])
    far, left, right, other, travel = lax.optimization_barrier((far, left, right, other, travel))

    other_left = ring(other, 1)
    other_right = ring(other, -1)
    other_far = across(far)
    row = [own, left, right, far]
    found, terms = correlate(row, travel, table, places_of(0), home_total)
    others = [other, other_left, other_right, other_far]
    found = correlate(others, terms, table, places_of(1), home_total, found)
    return found[None, None]


def solution(mesh):
    in_specs = (P(("pair", "freq"), None, None, None), P(("pair", "freq"), None, None, None), P())
    out_specs = P(None, "pair", None, "freq", None)
    return jax.shard_map(
        per_device, mesh=mesh, in_specs=in_specs, out_specs=out_specs, check_vma=False
    )
```

```python
import functools
import math

import jax
import jax.numpy as jnp
from jax import lax
from jax.experimental import pallas as pl
from jax.experimental.pallas import tpu as pltpu
from jax.sharding import PartitionSpec as P

LAGS = 128
BAND = 128
RUN = 8
PAD = 8


def make_table(freq_count, lag_count, window_count):
    freq_index = jnp.arange(freq_count, dtype=jnp.int32)[None, :]
    lag_index = jnp.arange(lag_count, dtype=jnp.int32)[:, None] - lag_count // 2
    phase_step = freq_index * lag_index % (2 * freq_count)
    angles = phase_step.astype(jnp.float32) * (math.pi / freq_count)
    norm_scale = 1.0 / math.sqrt(2.0 * window_count * freq_count)
    table = [jnp.cos(angles) * norm_scale, -jnp.sin(angles) * norm_scale]
    return jnp.concatenate(table, axis=1).astype(jnp.bfloat16)


def along(value, axis, by):
    count = lax.axis_size(axis)
    return lax.ppermute(value, axis, [(i, (i + by) % count) for i in range(count)])


def ring(value, step):
    return along(value, "freq", 2 * step)


def across(value):
    return lax.ppermute(value, "freq", [(i, i ^ 1) for i in range(lax.axis_size("freq"))])


def places_of(side):
    me = lax.axis_index("freq")
    place, row = me // 2, me % 2
    found = [((place + step) % 4) * 2 + (row ^ side) for step in (0, -1, 1, 2)]
    return jnp.stack(found).astype(jnp.int32)


def moved(value, by):
    count = lax.axis_size("pair")
    branch = lambda step: lambda v: along(v, "pair", step) if step else v
    return lax.switch(by, [branch(step) for step in range(count)], value)


def kernel(places, *refs, piece_count, first):
    pieces, travel, table = refs[:piece_count], refs[piece_count], refs[piece_count + 1]
    if first:
        out, terms, wide, weights, cross, turned, ready, sems = refs[piece_count + 2 :]
    else:
        terms = travel
        out, wide, weights, cross, turned, ready, sems = refs[piece_count + 3 :]
    _, term_count, band = pieces[0].shape
    channels, _, _, home_count = cross.shape
    half = term_count // 2
    groups = band // RUN
    lanes = term_count * RUN
    step = pl.program_id(0)

    pitch = term_count + PAD
    begin = 0
    for piece in pieces:
        for i in range(piece.shape[0]):
            wide[begin : begin + term_count] = piece[i].astype(jnp.float32)
            begin += pitch

    def of_term(k):
        rows = wide[pl.ds(k, home_count, stride=pitch), :]
        return rows.T.reshape(groups, RUN, home_count)

    for k in range(0, term_count, 2):
        two = jnp.concatenate([of_term(k), of_term(k + 1)], axis=1).astype(jnp.bfloat16)
        weights[:, k * RUN : (k + 2) * RUN, :home_count] = two
        if k < half:
            weights[:, (k + half) * RUN : (k + half + 2) * RUN, home_count:] = -two
        else:
            weights[:, (k - half) * RUN : (k - half + 2) * RUN, home_count:] = two

    if first:
        many = lanes // term_count
        blocks = channels // many
        sides = [travel[c : c + many].reshape(lanes, band).T for c in range(0, channels, many)]
        side = jnp.concatenate(sides, axis=0)
        spread_row = lax.broadcasted_iota(jnp.int32, (lanes, 2 * lanes), 0)
        spread_lane = lax.broadcasted_iota(jnp.int32, (lanes, 2 * lanes), 1)
        row = lax.broadcasted_iota(jnp.int32, (2 * RUN, lanes), 0)
        lane = lax.broadcasted_iota(jnp.int32, (2 * RUN, lanes), 1)
        diagonal = jnp.where(row % RUN == lane % RUN, 1.0, 0.0).astype(jnp.bfloat16)
        for j in range(many // 2):
            chosen = spread_row == 2 * j * term_count + spread_lane // RUN
            spread = jnp.where(chosen, 1.0, 0.0).astype(jnp.bfloat16)
            found = jnp.dot(side, spread, preferred_element_type=jnp.float32)
            found = found.reshape(blocks, groups, RUN, 2 * lanes)
            found = jnp.concatenate([found[..., :lanes], found[..., lanes:]], axis=2)
            found = found.astype(jnp.bfloat16) * diagonal
            for c in range(blocks):
                at = (c * many + 2 * j) * RUN
                terms[:, at : at + 2 * RUN, :] = found[c]

    for g in range(0, groups, 2):
        two = [
            jnp.dot(terms[g + i], weights[g + i], preferred_element_type=jnp.float32)
            for i in range(2)
        ]
        two = [x.reshape(channels, RUN, 2 * home_count) for x in two]
        found = jnp.concatenate(two, axis=1).astype(jnp.bfloat16)
        to = pl.ds(pl.multiple_of(step * band + g * RUN, 2 * RUN), 2 * RUN)
        cross[:, 0, to, :] = found[..., :home_count]
        cross[:, 1, to, :] = found[..., home_count:]

    @pl.when(step == pl.num_programs(0) - 1)
    def _():
        for t in range(0, channels, 2):
            two = [cross[t + i].reshape(-1, home_count) for i in range(2)]
            product = jnp.dot(
                table[...], jnp.concatenate(two, axis=1), preferred_element_type=jnp.float32
            )
            product = product.astype(jnp.bfloat16).T.astype(jnp.float32)
            for i in range(2):
                begin = (t + i) * (home_count + PAD)
                turned[begin : begin + home_count] = product[i * home_count : (i + 1) * home_count]
        block = home_count // piece_count
        copies = []
        for b in range(piece_count):

            def finish(i, carry):
                rows = turned[pl.ds(b * block + i, channels, stride=home_count + PAD), :]
                ready[b * block + i] = rows.astype(jnp.bfloat16)
                return carry

            lax.fori_loop(0, block, finish, 0, unroll=8)
            to = pl.ds(pl.multiple_of(places[b] * block, block), block)
            copies.append(
                pltpu.make_async_copy(ready.at[pl.ds(b * block, block)], out.at[to], sems.at[b])
            )
            copies[-1].start()
        for copy in copies:
            copy.wait()


def correlate(pieces, travel, table, places, home_total, so_far=None):
    first = so_far is None
    _, term_count, freq_count = pieces[0].shape
    home_count = sum(piece.shape[0] for piece in pieces)
    lag_count = table.shape[0]
    channels = travel.shape[0] if first else travel.shape[1] // RUN
    lanes = term_count * RUN
    spec = lambda n: pl.BlockSpec((n, term_count, BAND), lambda c: (0, 0, c))
    term_spec = pl.BlockSpec((BAND // RUN, channels * RUN, lanes), lambda c: (c, 0, 0))
    term_shape = jax.ShapeDtypeStruct((freq_count // RUN, channels * RUN, lanes), jnp.bfloat16)
    out_spec = pl.BlockSpec(memory_space=pl.ANY)
    out_shape = jax.ShapeDtypeStruct((home_total, channels, lag_count), jnp.bfloat16)
    earlier = [] if first else [so_far]
    return pl.pallas_call(
        functools.partial(kernel, piece_count=len(pieces), first=first),
        grid=(freq_count // BAND,),
        in_specs=[pl.BlockSpec(memory_space=pltpu.SMEM)]
        + [spec(piece.shape[0]) for piece in pieces]
        + [spec(channels) if first else term_spec]
        + [pl.BlockSpec((lag_count, 2 * freq_count), lambda c: (0, 0))]
        + [out_spec] * len(earlier),
        out_specs=[out_spec, term_spec] if first else out_spec,
        out_shape=[out_shape, term_shape] if first else out_shape,
        scratch_shapes=[
            pltpu.VMEM((home_count * (term_count + PAD), BAND), jnp.float32),
            pltpu.VMEM((BAND // RUN, lanes, 2 * home_count), jnp.bfloat16),
            pltpu.VMEM((channels, 2, freq_count, home_count), jnp.bfloat16),
            pltpu.VMEM(((home_count + PAD) * channels, lag_count), jnp.float32),
            pltpu.VMEM((home_count, channels, lag_count), jnp.bfloat16),
            pltpu.SemaphoreType.DMA((len(pieces),)),
        ],
        input_output_aliases={} if first else {len(pieces) + 3: 0},
        compiler_params=pltpu.CompilerParams(vmem_limit_bytes=32 * 2**20),
        cost_estimate=pl.CostEstimate(flops=10**6, bytes_accessed=10**5, transcendentals=0),
    )(places, *pieces, travel, table, *earlier)


def per_device(home_spectra, travel_spectra, rotation):
    own_count, parts, window_count, freq_count = home_spectra.shape
    home_total = own_count * lax.axis_size("freq")
    own = home_spectra.reshape(own_count, parts * window_count, freq_count)
    travel = travel_spectra.reshape(own_count, parts * window_count, freq_count)
    table = make_table(freq_count, LAGS, window_count)

    other = across(own)
    far = ring(own, 2)
    left = ring(own, 1)
    right = ring(own, -1)
    travel = moved(travel, rotation[0])
    other, far, left, right, travel = lax.optimization_barrier((other, far, left, right, travel))

    other_far = across(far)
    other_left = ring(other, 1)
    other_right = ring(other, -1)
    row = [own, left, right, far]
    found, terms = correlate(row, travel, table, places_of(0), home_total)
    others = [other, other_left, other_right, other_far]
    found = correlate(others, terms, table, places_of(1), home_total, found)
    return found[None, None]


def solution(mesh):
    in_specs = (P(("pair", "freq"), None, None, None), P(("pair", "freq"), None, None, None), P())
    out_specs = P(None, "pair", None, "freq", None)
    return jax.shard_map(
        per_device, mesh=mesh, in_specs=in_specs, out_specs=out_specs, check_vma=False
    )
```

```python
import functools
import math

import jax
import jax.numpy as jnp
from jax import lax
from jax.experimental import pallas as pl
from jax.experimental.pallas import tpu as pltpu
from jax.sharding import PartitionSpec as P

LAGS = 128
BAND = 128
RUN = 8
PAD = 8
BANDS = 2


def make_table(freq_count, lag_count, window_count):
    freq_index = jnp.arange(freq_count, dtype=jnp.int32)[None, :]
    lag_index = jnp.arange(lag_count, dtype=jnp.int32)[:, None] - lag_count // 2
    phase_step = freq_index * lag_index % (2 * freq_count)
    angles = phase_step.astype(jnp.float32) * (math.pi / freq_count)
    norm_scale = 1.0 / math.sqrt(2.0 * window_count * freq_count)
    table = [jnp.cos(angles) * norm_scale, -jnp.sin(angles) * norm_scale]
    return jnp.concatenate(table, axis=1).astype(jnp.bfloat16)


def along(value, axis, by):
    count = lax.axis_size(axis)
    return lax.ppermute(value, axis, [(i, (i + by) % count) for i in range(count)])


def ring(value, step):
    return along(value, "freq", 2 * step)


def across(value):
    return lax.ppermute(value, "freq", [(i, i ^ 1) for i in range(lax.axis_size("freq"))])


def places_of(side):
    me = lax.axis_index("freq")
    place, row = me // 2, me % 2
    found = [((place + step) % 4) * 2 + (row ^ side) for step in (0, -1, 1, 2)]
    return jnp.stack(found).astype(jnp.int32)


def moved(value, by):
    count = lax.axis_size("pair")
    branch = lambda step: lambda v: along(v, "pair", step) if step else v
    return lax.switch(by, [branch(step) for step in range(count)], value)


def kernel(places, *refs, piece_count, first):
    pieces, travel, table = refs[:piece_count], refs[piece_count], refs[piece_count + 1]
    if first:
        out, terms, wide, weights, cross, turned, ready, sems = refs[piece_count + 2 :]
    else:
        terms = travel
        out, wide, weights, cross, turned, ready, sems = refs[piece_count + 3 :]
    term_count, band = pieces[0].shape[1], wide.shape[2]
    channels, _, _, home_count = cross.shape
    half = term_count // 2
    groups = band // RUN
    lanes = term_count * RUN
    step = pl.program_id(0)

    pitch = term_count + PAD
    begin = 0
    for piece in pieces:
        for i in range(piece.shape[0]):
            for n in range(BANDS):
                rows = piece[i, :, n * band : (n + 1) * band].astype(jnp.float32)
                wide[n, begin : begin + term_count] = rows
            begin += pitch

    def of_term(n, k):
        rows = wide[n, pl.ds(k, home_count, stride=pitch), :]
        return rows.T.reshape(groups, RUN, home_count)

    def weigh(n, k):
        two = jnp.concatenate([of_term(n, k), of_term(n, k + 1)], axis=1).astype(jnp.bfloat16)
        weights[n, :, k * RUN : (k + 2) * RUN, :home_count] = two
        if k < half:
            weights[n, :, (k + half) * RUN : (k + half + 2) * RUN, home_count:] = -two
        else:
            weights[n, :, (k - half) * RUN : (k - half + 2) * RUN, home_count:] = two

    if first:
        many = lanes // term_count
        blocks = channels // many
        sides = [
            travel[c : c + many, :, n * band : (n + 1) * band].reshape(lanes, band).T
            for n in range(BANDS)
            for c in range(0, channels, many)
        ]
        side = jnp.concatenate(sides, axis=0)
        spread_row = lax.broadcasted_iota(jnp.int32, (lanes, 2 * lanes), 0)
        spread_lane = lax.broadcasted_iota(jnp.int32, (lanes, 2 * lanes), 1)
        row = lax.broadcasted_iota(jnp.int32, (2 * RUN, lanes), 0)
        lane = lax.broadcasted_iota(jnp.int32, (2 * RUN, lanes), 1)
        diagonal = jnp.where(row % RUN == lane % RUN, 1.0, 0.0).astype(jnp.bfloat16)
        for j in range(many // 2):
            chosen = spread_row == 2 * j * term_count + spread_lane // RUN
            spread = jnp.where(chosen, 1.0, 0.0).astype(jnp.bfloat16)
            found = jnp.dot(side, spread, preferred_element_type=jnp.float32)
            found = found.reshape(BANDS, blocks, groups, RUN, 2 * lanes)
            found = jnp.concatenate([found[..., :lanes], found[..., lanes:]], axis=3)
            found = found.astype(jnp.bfloat16) * diagonal
            for n in range(BANDS):
                for c in range(blocks):
                    at = (c * many + 2 * j) * RUN
                    terms[n * groups : (n + 1) * groups, at : at + 2 * RUN, :] = found[n, c]

    def multiply(n, g):
        two = [
            jnp.dot(
                terms[n * groups + g + i], weights[n, g + i], preferred_element_type=jnp.float32
            )
            for i in range(2)
        ]
        two = [x.reshape(channels, RUN, 2 * home_count) for x in two]
        found = jnp.concatenate(two, axis=1).astype(jnp.bfloat16)
        at = (step * BANDS + n) * band + g * RUN
        to = pl.ds(pl.multiple_of(at, 2 * RUN), 2 * RUN)
        cross[:, 0, to, :] = found[..., :home_count]
        cross[:, 1, to, :] = found[..., home_count:]

    for k in range(0, term_count, 2):
        weigh(0, k)
    for n in range(BANDS):
        for k in range(0, term_count, 2):
            if n + 1 < BANDS:
                weigh(n + 1, k)
            for g in range(k * groups // term_count, (k + 2) * groups // term_count, 2):
                multiply(n, g)

    @pl.when(step == pl.num_programs(0) - 1)
    def _():
        def transform(i, carry):
            two = [cross[2 * i + j].reshape(-1, home_count) for j in range(2)]
            product = jnp.dot(
                table[...], jnp.concatenate(two, axis=1), preferred_element_type=jnp.float32
            )
            product = product.astype(jnp.bfloat16).T.astype(jnp.float32)
            for j in range(2):
                begin = pl.multiple_of((2 * i + j) * (home_count + PAD), PAD)
                rows = product[j * home_count : (j + 1) * home_count]
                turned[pl.ds(begin, home_count)] = rows
            return carry

        lax.fori_loop(0, channels // 2, transform, 0, unroll=8)
        block = home_count // piece_count
        copies = []
        for b in range(piece_count):

            def finish(i, carry):
                rows = turned[pl.ds(b * block + i, channels, stride=home_count + PAD), :]
                ready[b * block + i] = rows.astype(jnp.bfloat16)
                return carry

            lax.fori_loop(0, block, finish, 0, unroll=8)
            to = pl.ds(pl.multiple_of(places[b] * block, block), block)
            copies.append(
                pltpu.make_async_copy(ready.at[pl.ds(b * block, block)], out.at[to], sems.at[b])
            )
            copies[-1].start()
        for copy in copies:
            copy.wait()


def correlate(pieces, travel, table, places, home_total, so_far=None):
    first = so_far is None
    _, term_count, freq_count = pieces[0].shape
    home_count = sum(piece.shape[0] for piece in pieces)
    lag_count = table.shape[0]
    channels = travel.shape[0] if first else travel.shape[1] // RUN
    lanes = term_count * RUN
    span = BANDS * BAND
    spec = lambda n: pl.BlockSpec((n, term_count, span), lambda c: (0, 0, c))
    term_spec = pl.BlockSpec((span // RUN, channels * RUN, lanes), lambda c: (c, 0, 0))
    term_shape = jax.ShapeDtypeStruct((freq_count // RUN, channels * RUN, lanes), jnp.bfloat16)
    out_spec = pl.BlockSpec(memory_space=pl.ANY)
    out_shape = jax.ShapeDtypeStruct((home_total, channels, lag_count), jnp.bfloat16)
    earlier = [] if first else [so_far]
    return pl.pallas_call(
        functools.partial(kernel, piece_count=len(pieces), first=first),
        grid=(freq_count // span,),
        in_specs=[pl.BlockSpec(memory_space=pltpu.SMEM)]
        + [spec(piece.shape[0]) for piece in pieces]
        + [spec(channels) if first else term_spec]
        + [pl.BlockSpec((lag_count, 2 * freq_count), lambda c: (0, 0))]
        + [out_spec] * len(earlier),
        out_specs=[out_spec, term_spec] if first else out_spec,
        out_shape=[out_shape, term_shape] if first else out_shape,
        scratch_shapes=[
            pltpu.VMEM((BANDS, home_count * (term_count + PAD), BAND), jnp.float32),
            pltpu.VMEM((BANDS, BAND // RUN, lanes, 2 * home_count), jnp.bfloat16),
            pltpu.VMEM((channels, 2, freq_count, home_count), jnp.bfloat16),
            pltpu.VMEM(((home_count + PAD) * channels, lag_count), jnp.float32),
            pltpu.VMEM((home_count, channels, lag_count), jnp.bfloat16),
            pltpu.SemaphoreType.DMA((len(pieces),)),
        ],
        input_output_aliases={} if first else {len(pieces) + 3: 0},
        compiler_params=pltpu.CompilerParams(vmem_limit_bytes=32 * 2**20),
        cost_estimate=pl.CostEstimate(flops=10**6, bytes_accessed=10**5, transcendentals=0),
    )(places, *pieces, travel, table, *earlier)


def per_device(home_spectra, travel_spectra, rotation):
    own_count, parts, window_count, freq_count = home_spectra.shape
    home_total = own_count * lax.axis_size("freq")
    own = home_spectra.reshape(own_count, parts * window_count, freq_count)
    travel = travel_spectra.reshape(own_count, parts * window_count, freq_count)
    table = make_table(freq_count, LAGS, window_count)

    other = across(own)
    far = ring(own, 2)
    left = ring(own, 1)
    right = ring(own, -1)
    travel = moved(travel, rotation[0])
    other, far, left, right, travel = lax.optimization_barrier((other, far, left, right, travel))

    other_far = across(far)
    other_left = ring(other, 1)
    other_right = ring(other, -1)
    row = [own, left, right, far]
    found, terms = correlate(row, travel, table, places_of(0), home_total)
    others = [other, other_left, other_right, other_far]
    found = correlate(others, terms, table, places_of(1), home_total, found)
    return found[None, None]


def solution(mesh):
    in_specs = (P(("pair", "freq"), None, None, None), P(("pair", "freq"), None, None, None), P())
    out_specs = P(None, "pair", None, "freq", None)
    return jax.shard_map(
        per_device, mesh=mesh, in_specs=in_specs, out_specs=out_specs, check_vma=False
    )
```

```python
import functools
import math

import jax
import jax.numpy as jnp
from jax import lax
from jax.experimental import pallas as pl
from jax.experimental.pallas import tpu as pltpu
from jax.sharding import PartitionSpec as P

LAGS = 128
BAND = 128
RUN = 8
PAD = 8
BANDS = 2


def make_table(freq_count, lag_count, window_count):
    freq_index = jnp.arange(freq_count, dtype=jnp.int32)[None, :]
    lag_index = jnp.arange(lag_count, dtype=jnp.int32)[:, None] - lag_count // 2
    phase_step = freq_index * lag_index % (2 * freq_count)
    angles = phase_step.astype(jnp.float32) * (math.pi / freq_count)
    norm_scale = 1.0 / math.sqrt(2.0 * window_count * freq_count)
    table = [jnp.cos(angles) * norm_scale, -jnp.sin(angles) * norm_scale]
    return jnp.concatenate(table, axis=1).astype(jnp.bfloat16)


def along(value, axis, by):
    count = lax.axis_size(axis)
    return lax.ppermute(value, axis, [(i, (i + by) % count) for i in range(count)])


def ring(value, step):
    return along(value, "freq", 2 * step)


def across(value):
    return lax.ppermute(value, "freq", [(i, i ^ 1) for i in range(lax.axis_size("freq"))])


def places_of(side):
    me = lax.axis_index("freq")
    place, row = me // 2, me % 2
    found = [((place + step) % 4) * 2 + (row ^ side) for step in (0, -1, 1, 2)]
    return jnp.stack(found).astype(jnp.int32)


def moved(value, by):
    count = lax.axis_size("pair")
    branch = lambda step: lambda v: along(v, "pair", step) if step else v
    return lax.switch(by, [branch(step) for step in range(count)], value)


def kernel(places, *refs, piece_count, first):
    pieces, travel, table = refs[:piece_count], refs[piece_count], refs[piece_count + 1]
    if first:
        out, terms, wide, weights, cross, turned, ready, sems = refs[piece_count + 2 :]
    else:
        terms = travel
        out, wide, weights, cross, turned, ready, sems = refs[piece_count + 3 :]
    term_count, band = pieces[0].shape[1], wide.shape[2]
    channels, _, _, home_count = cross.shape
    half = term_count // 2
    groups = band // RUN
    lanes = term_count * RUN
    step = pl.program_id(0)

    pitch = term_count + PAD
    begin = 0
    for piece in pieces:
        for i in range(piece.shape[0]):
            for n in range(BANDS):
                rows = piece[i, :, n * band : (n + 1) * band].astype(jnp.float32)
                wide[n, begin : begin + term_count] = rows
            begin += pitch

    def of_term(n, k):
        rows = wide[n, pl.ds(k, home_count, stride=pitch), :]
        return rows.T.reshape(groups, RUN, home_count)

    def weigh(n, k):
        two = jnp.concatenate([of_term(n, k), of_term(n, k + 1)], axis=1).astype(jnp.bfloat16)
        weights[n, :, k * RUN : (k + 2) * RUN, :home_count] = two
        if k < half:
            weights[n, :, (k + half) * RUN : (k + half + 2) * RUN, home_count:] = -two
        else:
            weights[n, :, (k - half) * RUN : (k - half + 2) * RUN, home_count:] = two

    if first:
        many = lanes // term_count
        blocks = channels // many
        sides = [
            travel[c : c + many, :, n * band : (n + 1) * band].reshape(lanes, band).T
            for n in range(BANDS)
            for c in range(0, channels, many)
        ]
        side = jnp.concatenate(sides, axis=0)
        spread_row = lax.broadcasted_iota(jnp.int32, (lanes, 2 * lanes), 0)
        spread_lane = lax.broadcasted_iota(jnp.int32, (lanes, 2 * lanes), 1)
        row = lax.broadcasted_iota(jnp.int32, (2 * RUN, lanes), 0)
        lane = lax.broadcasted_iota(jnp.int32, (2 * RUN, lanes), 1)
        diagonal = jnp.where(row % RUN == lane % RUN, 1.0, 0.0).astype(jnp.bfloat16)
        for j in range(many // 2):
            chosen = spread_row == 2 * j * term_count + spread_lane // RUN
            spread = jnp.where(chosen, 1.0, 0.0).astype(jnp.bfloat16)
            found = jnp.dot(side, spread, preferred_element_type=jnp.float32)
            found = found.reshape(BANDS, blocks, groups, RUN, 2 * lanes)
            found = jnp.concatenate([found[..., :lanes], found[..., lanes:]], axis=3)
            found = found.astype(jnp.bfloat16) * diagonal
            for n in range(BANDS):
                for c in range(blocks):
                    at = (c * many + 2 * j) * RUN
                    terms[n * groups : (n + 1) * groups, at : at + 2 * RUN, :] = found[n, c]

    def multiply(n, g):
        two = [
            jnp.dot(
                terms[n * groups + g + i], weights[n, g + i], preferred_element_type=jnp.float32
            )
            for i in range(2)
        ]
        two = [x.reshape(channels, RUN, 2 * home_count) for x in two]
        found = jnp.concatenate(two, axis=1).astype(jnp.bfloat16)
        at = (step * BANDS + n) * band + g * RUN
        to = pl.ds(pl.multiple_of(at, 2 * RUN), 2 * RUN)
        cross[:, 0, to, :] = found[..., :home_count]
        cross[:, 1, to, :] = found[..., home_count:]

    for k in range(0, term_count, 2):
        weigh(0, k)
    for n in range(BANDS):
        for k in range(0, term_count, 2):
            if n + 1 < BANDS:
                weigh(n + 1, k)
            for g in range(k * groups // term_count, (k + 2) * groups // term_count, 2):
                multiply(n, g)

    @pl.when(step == pl.num_programs(0) - 1)
    def _():
        def transform(i, carry):
            two = [cross[2 * i + j].reshape(-1, home_count) for j in range(2)]
            product = jnp.dot(
                table[...], jnp.concatenate(two, axis=1), preferred_element_type=jnp.float32
            )
            product = product.astype(jnp.bfloat16).T.astype(jnp.float32)
            for j in range(2):
                begin = pl.multiple_of((2 * i + j) * (home_count + PAD), PAD)
                rows = product[j * home_count : (j + 1) * home_count]
                turned[pl.ds(begin, home_count)] = rows
            return carry

        lax.fori_loop(0, channels // 2, transform, 0, unroll=8)
        block = home_count // piece_count
        copies = []
        for b in range(piece_count):

            def finish(i, carry):
                rows = turned[pl.ds(b * block + i, channels, stride=home_count + PAD), :]
                ready[b * block + i] = rows.astype(jnp.bfloat16)
                return carry

            lax.fori_loop(0, block, finish, 0, unroll=8)
            to = pl.ds(pl.multiple_of(places[b] * block, block), block)
            copies.append(
                pltpu.make_async_copy(ready.at[pl.ds(b * block, block)], out.at[to], sems.at[b])
            )
            copies[-1].start()
        for copy in copies:
            copy.wait()


def correlate(pieces, travel, table, places, home_total, so_far=None):
    first = so_far is None
    _, term_count, freq_count = pieces[0].shape
    home_count = sum(piece.shape[0] for piece in pieces)
    lag_count = table.shape[0]
    channels = travel.shape[0] if first else travel.shape[1] // RUN
    lanes = term_count * RUN
    span = BANDS * BAND
    spec = lambda n: pl.BlockSpec((n, term_count, span), lambda c: (0, 0, c))
    term_spec = pl.BlockSpec((span // RUN, channels * RUN, lanes), lambda c: (c, 0, 0))
    term_shape = jax.ShapeDtypeStruct((freq_count // RUN, channels * RUN, lanes), jnp.bfloat16)
    out_spec = pl.BlockSpec(memory_space=pl.ANY)
    out_shape = jax.ShapeDtypeStruct((home_total, channels, lag_count), jnp.bfloat16)
    earlier = [] if first else [so_far]
    return pl.pallas_call(
        functools.partial(kernel, piece_count=len(pieces), first=first),
        grid=(freq_count // span,),
        in_specs=[pl.BlockSpec(memory_space=pltpu.SMEM)]
        + [spec(piece.shape[0]) for piece in pieces]
        + [spec(channels) if first else term_spec]
        + [pl.BlockSpec((lag_count, 2 * freq_count), lambda c: (0, 0))]
        + [out_spec] * len(earlier),
        out_specs=[out_spec, term_spec] if first else out_spec,
        out_shape=[out_shape, term_shape] if first else out_shape,
        scratch_shapes=[
            pltpu.VMEM((BANDS, home_count * (term_count + PAD), BAND), jnp.float32),
            pltpu.VMEM((BANDS, BAND // RUN, lanes, 2 * home_count), jnp.bfloat16),
            pltpu.VMEM((channels, 2, freq_count, home_count), jnp.bfloat16),
            pltpu.VMEM(((home_count + PAD) * channels, lag_count), jnp.float32),
            pltpu.VMEM((home_count, channels, lag_count), jnp.bfloat16),
            pltpu.SemaphoreType.DMA((len(pieces),)),
        ],
        input_output_aliases={} if first else {len(pieces) + 3: 0},
        compiler_params=pltpu.CompilerParams(vmem_limit_bytes=32 * 2**20),
        cost_estimate=pl.CostEstimate(flops=10**6, bytes_accessed=10**5, transcendentals=0),
    )(places, *pieces, travel, table, *earlier)


def per_device(home_spectra, travel_spectra, rotation):
    own_count, parts, window_count, freq_count = home_spectra.shape
    home_total = own_count * lax.axis_size("freq")
    own = home_spectra.reshape(own_count, parts * window_count, freq_count)
    travel = travel_spectra.reshape(own_count, parts * window_count, freq_count)
    table = make_table(freq_count, LAGS, window_count)

    other = across(own)
    far = ring(own, 2)
    left = ring(own, 1)
    right = ring(own, -1)
    travel = moved(travel, rotation[0])
    other, travel = lax.optimization_barrier((other, travel))

    other_far = across(far)
    other_left = ring(other, 1)
    other_right = ring(other, -1)
    row = [own, left, right, far]
    found, terms = correlate(row, travel, table, places_of(0), home_total)
    others = [other, other_left, other_right, other_far]
    found = correlate(others, terms, table, places_of(1), home_total, found)
    return found[None, None]


def solution(mesh):
    in_specs = (P(("pair", "freq"), None, None, None), P(("pair", "freq"), None, None, None), P())
    out_specs = P(None, "pair", None, "freq", None)
    return jax.shard_map(
        per_device, mesh=mesh, in_specs=in_specs, out_specs=out_specs, check_vma=False
    )
```

```python
import functools
import math

import jax
import jax.numpy as jnp
from jax import lax
from jax.experimental import pallas as pl
from jax.experimental.pallas import tpu as pltpu
from jax.sharding import PartitionSpec as P

LAGS = 128
BAND = 128
RUN = 8
PAD = 8


def make_table(freq_count, lag_count, window_count):
    freq_index = jnp.arange(freq_count, dtype=jnp.int32)[None, :]
    lag_index = jnp.arange(lag_count, dtype=jnp.int32)[:, None] - lag_count // 2
    phase_step = freq_index * lag_index % (2 * freq_count)
    angles = phase_step.astype(jnp.float32) * (math.pi / freq_count)
    norm_scale = 1.0 / math.sqrt(2.0 * window_count * freq_count)
    table = [jnp.cos(angles) * norm_scale, -jnp.sin(angles) * norm_scale]
    return jnp.concatenate(table, axis=1).astype(jnp.bfloat16)


def along(value, axis, by):
    count = lax.axis_size(axis)
    return lax.ppermute(value, axis, [(i, (i + by) % count) for i in range(count)])


def ring(value, step):
    return along(value, "freq", 2 * step)


def across(value):
    return lax.ppermute(value, "freq", [(i, i ^ 1) for i in range(lax.axis_size("freq"))])


def places_of(side):
    me = lax.axis_index("freq")
    place, row = me // 2, me % 2
    found = [((place + step) % 4) * 2 + (row ^ side) for step in (0, -1, 1, 2)]
    return jnp.stack(found).astype(jnp.int32)


def moved(value, by):
    count = lax.axis_size("pair")
    branch = lambda step: lambda v: along(v, "pair", step) if step else v
    return lax.switch(by, [branch(step) for step in range(count)], value)


def kernel(places, *refs, piece_count, first, bands):
    pieces, travel, table = refs[:piece_count], refs[piece_count], refs[piece_count + 1]
    if first:
        out, terms, wide, weights, cross, turned, ready, sems = refs[piece_count + 2 :]
    else:
        terms = travel
        out, wide, weights, cross, turned, ready, sems = refs[piece_count + 3 :]
    term_count, band = pieces[0].shape[1], wide.shape[2]
    channels, _, _, home_count = cross.shape
    half = term_count // 2
    groups = band // RUN
    lanes = term_count * RUN
    step = pl.program_id(0)

    pitch = term_count + PAD
    begin = 0
    for piece in pieces:
        for i in range(piece.shape[0]):
            for n in range(bands):
                rows = piece[i, :, n * band : (n + 1) * band].astype(jnp.float32)
                wide[n, begin : begin + term_count] = rows
            begin += pitch

    def of_term(n, k):
        rows = wide[n, pl.ds(k, home_count, stride=pitch), :]
        return rows.T.reshape(groups, RUN, home_count)

    def weigh(n, k):
        two = jnp.concatenate([of_term(n, k), of_term(n, k + 1)], axis=1).astype(jnp.bfloat16)
        weights[n, :, k * RUN : (k + 2) * RUN, :home_count] = two
        if k < half:
            weights[n, :, (k + half) * RUN : (k + half + 2) * RUN, home_count:] = -two
        else:
            weights[n, :, (k - half) * RUN : (k - half + 2) * RUN, home_count:] = two

    if first:
        many = lanes // term_count
        blocks = channels // many
        sides = [
            travel[c : c + many, :, n * band : (n + 1) * band].reshape(lanes, band).T
            for n in range(bands)
            for c in range(0, channels, many)
        ]
        side = jnp.concatenate(sides, axis=0)
        spread_row = lax.broadcasted_iota(jnp.int32, (lanes, 2 * lanes), 0)
        spread_lane = lax.broadcasted_iota(jnp.int32, (lanes, 2 * lanes), 1)
        row = lax.broadcasted_iota(jnp.int32, (2 * RUN, lanes), 0)
        lane = lax.broadcasted_iota(jnp.int32, (2 * RUN, lanes), 1)
        diagonal = jnp.where(row % RUN == lane % RUN, 1.0, 0.0).astype(jnp.bfloat16)
        for j in range(many // 2):
            chosen = spread_row == 2 * j * term_count + spread_lane // RUN
            spread = jnp.where(chosen, 1.0, 0.0).astype(jnp.bfloat16)
            found = jnp.dot(side, spread, preferred_element_type=jnp.float32)
            found = found.reshape(bands, blocks, groups, RUN, 2 * lanes)
            found = jnp.concatenate([found[..., :lanes], found[..., lanes:]], axis=3)
            found = found.astype(jnp.bfloat16) * diagonal
            for n in range(bands):
                for c in range(blocks):
                    at = (c * many + 2 * j) * RUN
                    terms[n * groups : (n + 1) * groups, at : at + 2 * RUN, :] = found[n, c]

    def multiply(n, g):
        two = [
            jnp.dot(
                terms[n * groups + g + i], weights[n, g + i], preferred_element_type=jnp.float32
            )
            for i in range(2)
        ]
        two = [x.reshape(channels, RUN, 2 * home_count) for x in two]
        found = jnp.concatenate(two, axis=1).astype(jnp.bfloat16)
        at = (step * bands + n) * band + g * RUN
        to = pl.ds(pl.multiple_of(at, 2 * RUN), 2 * RUN)
        cross[:, 0, to, :] = found[..., :home_count]
        cross[:, 1, to, :] = found[..., home_count:]

    for k in range(0, term_count, 2):
        weigh(0, k)
    for n in range(bands):
        for k in range(0, term_count, 2):
            if n + 1 < bands:
                weigh(n + 1, k)
            for g in range(k * groups // term_count, (k + 2) * groups // term_count, 2):
                multiply(n, g)

    @pl.when(step == pl.num_programs(0) - 1)
    def _():
        def transform(i, carry):
            two = [cross[2 * i + j].reshape(-1, home_count) for j in range(2)]
            product = jnp.dot(
                table[...], jnp.concatenate(two, axis=1), preferred_element_type=jnp.float32
            )
            product = product.astype(jnp.bfloat16).T.astype(jnp.float32)
            for j in range(2):
                begin = pl.multiple_of((2 * i + j) * (home_count + PAD), PAD)
                rows = product[j * home_count : (j + 1) * home_count]
                turned[pl.ds(begin, home_count)] = rows
            return carry

        lax.fori_loop(0, channels // 2, transform, 0, unroll=8)
        block = home_count // piece_count
        copies = []
        for b in range(piece_count):

            def finish(i, carry):
                rows = turned[pl.ds(b * block + i, channels, stride=home_count + PAD), :]
                ready[b * block + i] = rows.astype(jnp.bfloat16)
                return carry

            lax.fori_loop(0, block, finish, 0, unroll=8)
            to = pl.ds(pl.multiple_of(places[b] * block, block), block)
            copies.append(
                pltpu.make_async_copy(ready.at[pl.ds(b * block, block)], out.at[to], sems.at[b])
            )
            copies[-1].start()
        for copy in copies:
            copy.wait()


def correlate(pieces, travel, table, places, home_total, so_far=None):
    first = so_far is None
    _, term_count, freq_count = pieces[0].shape
    bands = 1 if first else freq_count // BAND
    home_count = sum(piece.shape[0] for piece in pieces)
    lag_count = table.shape[0]
    channels = travel.shape[0] if first else travel.shape[1] // RUN
    lanes = term_count * RUN
    span = bands * BAND
    spec = lambda n: pl.BlockSpec((n, term_count, span), lambda c: (0, 0, c))
    term_spec = pl.BlockSpec((span // RUN, channels * RUN, lanes), lambda c: (c, 0, 0))
    term_shape = jax.ShapeDtypeStruct((freq_count // RUN, channels * RUN, lanes), jnp.bfloat16)
    out_spec = pl.BlockSpec(memory_space=pl.ANY)
    out_shape = jax.ShapeDtypeStruct((home_total, channels, lag_count), jnp.bfloat16)
    earlier = [] if first else [so_far]
    return pl.pallas_call(
        functools.partial(kernel, piece_count=len(pieces), first=first, bands=bands),
        grid=(freq_count // span,),
        in_specs=[pl.BlockSpec(memory_space=pltpu.SMEM)]
        + [spec(piece.shape[0]) for piece in pieces]
        + [spec(channels) if first else term_spec]
        + [pl.BlockSpec((lag_count, 2 * freq_count), lambda c: (0, 0))]
        + [out_spec] * len(earlier),
        out_specs=[out_spec, term_spec] if first else out_spec,
        out_shape=[out_shape, term_shape] if first else out_shape,
        scratch_shapes=[
            pltpu.VMEM((bands, home_count * (term_count + PAD), BAND), jnp.float32),
            pltpu.VMEM((bands, BAND // RUN, lanes, 2 * home_count), jnp.bfloat16),
            pltpu.VMEM((channels, 2, freq_count, home_count), jnp.bfloat16),
            pltpu.VMEM(((home_count + PAD) * channels, lag_count), jnp.float32),
            pltpu.VMEM((home_count, channels, lag_count), jnp.bfloat16),
            pltpu.SemaphoreType.DMA((len(pieces),)),
        ],
        input_output_aliases={} if first else {len(pieces) + 3: 0},
        compiler_params=pltpu.CompilerParams(vmem_limit_bytes=42 * 2**20),
        cost_estimate=pl.CostEstimate(flops=10**6, bytes_accessed=10**5, transcendentals=0),
    )(places, *pieces, travel, table, *earlier)


def per_device(home_spectra, travel_spectra, rotation):
    own_count, parts, window_count, freq_count = home_spectra.shape
    home_total = own_count * lax.axis_size("freq")
    own = home_spectra.reshape(own_count, parts * window_count, freq_count)
    travel = travel_spectra.reshape(own_count, parts * window_count, freq_count)
    table = make_table(freq_count, LAGS, window_count)

    other = across(own)
    far = ring(own, 2)
    left = ring(own, 1)
    right = ring(own, -1)
    travel = moved(travel, rotation[0])
    other, travel = lax.optimization_barrier((other, travel))

    other_far = across(far)
    other_left = ring(other, 1)
    other_right = ring(other, -1)
    row = [own, left, right, far]
    found, terms = correlate(row, travel, table, places_of(0), home_total)
    others = [other, other_left, other_right, other_far]
    found = correlate(others, terms, table, places_of(1), home_total, found)
    return found[None, None]


def solution(mesh):
    in_specs = (P(("pair", "freq"), None, None, None), P(("pair", "freq"), None, None, None), P())
    out_specs = P(None, "pair", None, "freq", None)
    return jax.shard_map(
        per_device, mesh=mesh, in_specs=in_specs, out_specs=out_specs, check_vma=False
    )
```
